32 devices in a mesh: expert: 16 (over z, y, x), dp: 2 (over core).
Axes of the slice: x: 2, y: 2, z: 4, core: 2. Of those that a mesh axis runs over, the one named last changes fastest.
Arguments:
- tokens: bfloat16 [4096, 2048], P(('dp', 'expert')), parts along dimension 0, may hold values from -6 to 6
- route_ids: int32 [4096, 8], P(('dp', 'expert')), parts along dimension 0, may hold values from 0 to 15, all different within a row; in each aligned block of 128 rows (0 to 127, 128 to 255, ...) at most 80 rows name the same one
- route_weights: float32 [4096, 8], P(('dp', 'expert')), parts along dimension 0, may hold values from 0.05 to 0.3
- w_gate: bfloat16 [16, 2048, 768], P(None, 'expert'), may hold values from -0.125 to 0.125
- w_up: bfloat16 [16, 2048, 768], P(None, 'expert'), may hold values from -0.125 to 0.125
- w_down: bfloat16 [16, 768, 2048], P(None, 'expert'), may hold values from -0.21875 to 0.21875
Outputs:
- moe_output: bfloat16 [4096, 2048], P(('dp', 'expert')), parts along dimension 0
The draws below stay inside these ranges and needn't reach their ends.
There are 2 independent parts, one for each index of `dp`. The reference program is written for one: setup_inputs(seed, part) draws one part's arguments, and reference() takes and returns one part's arrays. A program takes and returns all parts, laid end to end along the dimension named above; an argument that names none is the same for every part. Nothing has to cross between parts.
Inputs may be any that keep to these rules, and one draw needn't show every extreme that they name: `route_ids`: each token names 8 different experts. Within each aligned block of 128 tokens no expert is named by more than 80 routes, and in some block some expert is named by exactly 80 routes.
All inputs are finite; a program needn't handle non-finite values.
Results may differ from the reference program's by a relative error of at most 0.0057.
Values may be sent and summed in bfloat16 or wider, within the bound.
No kernel may reach another device: no remote copies, remote signals or barrier semaphores. Data moves between devices by JAX's collectives and lax.ppermute only.
A program may use at most 128 MiB of HBM per device.

```python
import math
import jax
import jax.numpy as jnp
import numpy as np
from jax import lax

D = 2048
F = 768
TOPK = 8
TOK_DEV = 128
EXPERTS = 16
TOKENS = 2048
CAP = 80


def block_levels(stream_key, extent, pieces, low, high):
    factor_of, own = 1.0, jax.random.fold_in(stream_key, 6)
    for dim, parts in pieces:
        draws = jnp.exp(jax.random.uniform(jax.random.fold_in(own, dim), (parts,), jnp.float32, low / len(pieces), high / len(pieces)))
        factor_of = factor_of * jnp.repeat(draws, extent[dim] // parts).reshape([-1 if axis == dim else 1 for axis in range(len(extent))])
    return factor_of


def deal_out(key, own, number, rows, count, top, reach, skew):
    ranking = jax.random.permutation(key, count)
    crowded, ordinary = load_shares(count, rows * top, reach, skew, True), load_shares(count, rows * top, reach, skew, False)
    places = jnp.arange(count)

    def named(tallies, turn):
        used = int((tallies > 0).sum())
        fixed = max(1, used // 4)
        shifted = fixed + (places - fixed + turn * (used - fixed)) % max(1, count - fixed)
        return jnp.zeros((count,), jnp.int32).at[ranking[jnp.where(places < fixed, places, shifted)]].set(jnp.asarray(tallies, jnp.int32))

    tallies = jnp.where(number % 4 == 0, named(crowded, number // 4), named(ordinary, number - number // 4 - 1))
    mixed = jax.random.permutation(jax.random.fold_in(own, 3), count)
    giver, taker = mixed[0:count // 2 * 2:2], mixed[1:count // 2 * 2:2]
    margin = jnp.minimum(tallies[giver] - 1, reach - tallies[taker]) // 2
    margin = jnp.where((giver == ranking[0]) | (taker == ranking[0]) | (tallies[taker] == 0), 0, jnp.maximum(margin, 0))
    shifted = jax.random.randint(jax.random.fold_in(own, 4), (count // 2,), 0, 1 << 20) % (margin + 1)
    tallies = tallies.at[giver].add(-shifted).at[taker].add(shifted)
    members = jnp.searchsorted(jnp.cumsum(tallies), jnp.arange(rows * top), side="right").astype(jnp.int32)
    table = members.reshape(top, rows).T
    table = table[jax.random.permutation(jax.random.fold_in(own, 1), rows)]
    turn = jax.random.randint(jax.random.fold_in(own, 2), (rows, 1), 0, top)
    return jnp.take_along_axis(table, (jnp.arange(top)[None, :] + turn) % top, axis=1)


def load_shares(amount, total, bound, skew, full):
    loads = [(1 << 20) // math.isqrt(standing ** skew) + 1 for standing in range(1, amount + 1)]
    largest = bound if full else min(bound, max(-(-total // amount), total * loads[0] // sum(loads)))
    least = 1 if total - largest >= amount - 1 else 0
    counts, rest = [largest] + [least] * (amount - 1), total - largest - least * (amount - 1)
    while rest > 0:
        free = [i for i in range(1, amount) if counts[i] < largest] or [i for i in range(1, amount) if counts[i] < bound]
        pool, left = sum([loads[i] for i in free]), rest
        for i in free:
            extra = min(bound - counts[i], max(1, left * loads[i] // pool), rest)
            counts[i] = counts[i] + extra
            rest = rest - extra
    return np.array(counts)


def bell_draw(stream_key, dims, width, reach, shards=(), held_as=jnp.bfloat16):
    level = block_levels(stream_key, dims, shards, -0.22, 0.18) if shards else 1.0
    result = jax.random.normal(stream_key, dims, jnp.float32) * width * level
    return jnp.minimum(jnp.maximum(result, -reach), reach).astype(held_as)


def setup_inputs(seed: int = 0, part: int = 0) -> dict:
    key_of = jax.random.split(jax.random.key(seed), 7)
    own_keys = jax.random.split(jax.random.fold_in(key_of[6], part), 7)
    tokens = bell_draw(own_keys[0], (TOKENS, D), 1.0, 6.0, ((0, 16),))
    route_ids_keys = jax.random.split(jax.random.fold_in(own_keys[1], 1), TOKENS // TOK_DEV)
    route_ids_turns = jax.random.permutation(jax.random.fold_in(own_keys[1], 3), TOKENS // TOK_DEV)
    route_ids = jax.vmap(lambda own, number: deal_out(jax.random.fold_in(own_keys[1], 2), own, number, TOK_DEV, EXPERTS, TOPK, CAP, 2))(route_ids_keys, route_ids_turns).reshape((TOKENS, TOPK))
    route_weights = jnp.clip(0.05 + 0.25 * jax.random.uniform(own_keys[2], (TOKENS, TOPK), jnp.float32) ** block_levels(own_keys[2], (TOKENS, TOPK), ((0, 16),), -0.2, 0.2), 0.05, 0.3)
    w_gate = bell_draw(key_of[3], (EXPERTS, D, F), D ** -0.5, 0.125, ((1, 16),))
    w_up = bell_draw(key_of[4], (EXPERTS, D, F), D ** -0.5, 0.125, ((1, 16),))
    w_down = bell_draw(key_of[5], (EXPERTS, F, D), F ** -0.5, 0.21875, ((1, 16),))
    return dict(tokens=tokens, route_ids=route_ids, route_weights=route_weights, w_gate=w_gate, w_up=w_up, w_down=w_down)


def slots_of(block_ids):
    route_flat = block_ids.reshape(-1).astype(jnp.int32)
    one_hot = (route_flat[:, None] == jnp.arange(EXPERTS, dtype=jnp.int32)[None, :]).astype(jnp.int32)
    earlier = jnp.cumsum(one_hot, axis=0) - one_hot
    position = jnp.sum(earlier * one_hot, axis=1).astype(jnp.int32)
    return (route_flat * CAP + position).reshape(block_ids.shape).astype(jnp.int32)


def build_block(inputs):
    token_rows, slot_rows = inputs
    source = jnp.repeat(jnp.arange(TOK_DEV, dtype=jnp.int32), TOPK)
    buffer = jnp.zeros((EXPERTS * CAP, D), jnp.bfloat16)
    return buffer.at[slot_rows.reshape(-1)].set(token_rows[source])


def serve_expert(inputs):
    expert_rows, gate_rows, up_rows, down_rows = inputs
    gate_proj = jnp.dot(expert_rows, gate_rows, preferred_element_type=jnp.float32)
    up_proj = jnp.dot(expert_rows, up_rows, preferred_element_type=jnp.float32)
    hidden = (jax.nn.silu(gate_proj) * up_proj).astype(jnp.bfloat16)
    return jnp.dot(hidden, down_rows, preferred_element_type=jnp.float32).astype(jnp.bfloat16)


def combine_block(inputs):
    block_out, slot_rows, weight_rows = inputs
    picked = block_out[slot_rows]
    return jnp.sum(weight_rows[:, :, None] * picked.astype(jnp.float32), axis=1).astype(jnp.bfloat16)


def reference(tokens, route_ids, route_weights, w_gate, w_up, w_down):
    blocks = TOKENS // TOK_DEV
    slots = lax.map(slots_of, route_ids.reshape(blocks, TOK_DEV, TOPK))
    dispatched = lax.map(build_block, (tokens.reshape(blocks, TOK_DEV, D), slots))
    by_expert = dispatched.reshape(blocks, EXPERTS, CAP, D).transpose(1, 0, 2, 3).reshape(EXPERTS, blocks * CAP, D)
    expert_out = lax.map(serve_expert, (by_expert, w_gate, w_up, w_down))
    by_block = expert_out.reshape(EXPERTS, blocks, CAP, D).transpose(1, 0, 2, 3).reshape(blocks, EXPERTS * CAP, D)
    mixed = lax.map(combine_block, (by_block, slots, route_weights.reshape(blocks, TOK_DEV, TOPK)))
    return mixed.reshape(TOKENS, D)
```

```python
import jax
import jax.numpy as jnp
from jax import lax
from jax.sharding import PartitionSpec as P


def swap_cores(x):
    size = lax.axis_size("dp")
    return lax.ppermute(x, "dp", [(i, i ^ 1) for i in range(size)])


def flip(x, bit):
    size = lax.axis_size("expert")
    return lax.ppermute(x, "expert", [(i, i ^ bit) for i in range(size)])


def turn(x, by):
    size = lax.axis_size("expert")
    return lax.ppermute(x, "expert", [(i, (i + 4 * by) % size) for i in range(size)])


def local(tokens, route_ids, route_weights, w_gate, w_up, w_down):
    devices = lax.axis_size("expert")
    experts, depth, width = w_gate.shape
    rows, model = tokens.shape
    line = devices // 4
    me = lax.axis_index("expert")
    core = lax.axis_index("dp") % 2
    half, part = width // 2, model // 2

    def sliced(w, size):
        return lax.dynamic_slice_in_dim(w, core * size, size, axis=2)

    wide = jnp.concatenate([sliced(w_gate, half), sliced(w_up, half)], axis=2)
    wide = lax.all_to_all(wide, "expert", split_axis=0, concat_axis=0, tiled=True)
    wide = wide.reshape(devices * depth, width)
    wide_other = swap_cores(wide)
    down = lax.all_to_all(sliced(w_down, part), "expert", split_axis=0, concat_axis=0, tiled=True)
    down = down.reshape(width, part)
    down_other = swap_cores(down)

    share = jnp.sum(
        jnp.where(
            route_ids[None, :, :] == jnp.arange(experts, dtype=jnp.int32)[:, None, None],
            route_weights[None, :, :],
            0.0,
        ),
        axis=2,
    )
    shares = lax.all_gather(share, "expert", axis=0)
    mine = lax.dynamic_index_in_dim(shares, me, axis=1, keepdims=False)
    order = jnp.array(
        [[((me // 4 - s) % line) * 4 + ((me % 4) ^ q) for q in range(4)] for s in range(line)]
    )
    mine = mine[order.reshape(-1)].reshape(line, 4 * rows)

    held = [tokens]
    for _ in range(line - 1):
        held.append(turn(held[-1], 1))
    blocks = []
    for s in range(line):
        by_x, by_y = flip(held[s], 1), flip(held[s], 2)
        across = jnp.concatenate([flip(by_x[:, :part], 2), flip(by_y[:, part:], 1)], axis=1)
        blocks.append(jnp.concatenate([held[s], by_x, by_y, across], axis=0))

    def hidden_of(x, w):
        both = jnp.dot(x, w, preferred_element_type=jnp.float32)
        return (jax.nn.silu(both[:, :half]) * both[:, half:]).astype(jnp.bfloat16)

    arriving = None
    for s in reversed(range(line)):
        own, other = hidden_of(blocks[s], wide), hidden_of(blocks[s], wide_other)
        hidden = jnp.where(
            core == 0, jnp.concatenate([own, other], axis=1), jnp.concatenate([other, own], axis=1)
        )
        scale = mine[s][:, None]
        outs = [
            (jnp.dot(hidden, w, preferred_element_type=jnp.float32) * scale).astype(jnp.bfloat16)
            for w in (down, down_other)
        ]
        near, by_x, by_y, across = zip(*[[o[q * rows : (q + 1) * rows] for q in range(4)] for o in outs])
        f32 = jnp.float32
        x0 = (by_x[0].astype(f32) + flip(across[0], 2).astype(f32)).astype(jnp.bfloat16)
        y1 = (by_y[1].astype(f32) + flip(across[1], 1).astype(f32)).astype(jnp.bfloat16)
        from_x = flip(jnp.concatenate([x0, by_x[1]], axis=1), 1)
        from_y = flip(jnp.concatenate([by_y[0], y1], axis=1), 2)
        total = jnp.concatenate(near, axis=1).astype(f32) + from_x.astype(f32) + from_y.astype(f32)
        if arriving is not None:
            total = total + arriving.astype(f32)
        if s > 0:
            arriving = turn(total.astype(jnp.bfloat16), -1)
    left, right = total[:, :part], total[:, part:]
    result = jnp.where(
        core == 0, jnp.concatenate([left, right], axis=1), jnp.concatenate([right, left], axis=1)
    )
    return result.astype(jnp.bfloat16)


def solution(mesh):
    placed = (
        P(("dp", "expert"), None),
        P(("dp", "expert"), None),
        P(("dp", "expert"), None),
        P(None, "expert", None),
        P(None, "expert", None),
        P(None, "expert", None),
    )
    return jax.shard_map(
        local, mesh=mesh, in_specs=placed, out_specs=P(("dp", "expert"), None), check_vma=False
    )
```

```python
import functools

import jax
import jax.numpy as jnp
from jax import lax
from jax.experimental import pallas as pl
from jax.experimental.pallas import tpu as pltpu
from jax.sharding import PartitionSpec as P

PIECES = 1


def swap_cores(x):
    size = lax.axis_size("dp")
    return lax.ppermute(x, "dp", [(i, i ^ 1) for i in range(size)])


def flip(x, bit):
    size = lax.axis_size("expert")
    return lax.ppermute(x, "expert", [(i, i ^ bit) for i in range(size)])


def turn(x, by):
    size = lax.axis_size("expert")
    return lax.ppermute(x, "expert", [(i, (i + 4 * by) % size) for i in range(size)])


def spread(w):
    return lax.all_to_all(w, "expert", split_axis=0, concat_axis=0, tiled=True)


def after(x, *others):
    return lax.optimization_barrier((x, *others))[0]


def hidden_kernel(blocks, rows, model, experts, place, *refs):
    tokens, weights = refs[:blocks], refs[blocks : blocks + 2 * PIECES]
    hidden, scale = refs[blocks + 2 * PIECES : blocks + 2 * PIECES + 2]
    held, loaded, token_sems, weight_sems = refs[blocks + 2 * PIECES + 2 :]
    me, core = place[0], place[1]
    token_copies = [
        pltpu.make_async_copy(tokens[i], held.at[pl.ds(i * rows, rows)], token_sems.at[i]) for i in range(blocks)
    ]
    weight_copies = [
        pltpu.make_async_copy(weights[i], loaded.at[i], weight_sems.at[i]) for i in range(2 * PIECES)
    ]
    for i in range(4):
        token_copies[i].start()
    for copy in weight_copies:
        copy.start()
    for i in range(4, blocks):
        token_copies[i].start()
    for i in range(4):
        token_copies[i].wait()
    for copy in weight_copies:
        copy.wait()
    for i in range(4, blocks):
        token_copies[i].wait()
    group = 4 * rows
    piece = loaded.shape[2] // 2
    columns = held.shape[1] - model

    def step(s, carry):
        at = pl.ds(pl.multiple_of(s * group, group), group)
        lane = lax.broadcasted_iota(jnp.int32, (group, columns), 1)
        wanted = (lane == me) | (lane == me + experts) | (lane == me + 2 * experts)
        picked = jnp.where(wanted, held[at, model:].astype(jnp.float32), 0.0)
        scale[at, :] = jnp.broadcast_to(jnp.sum(picked, axis=1, keepdims=True), (group, 128))
        x = held[at, :model]
        for side in range(2):
            start = jnp.where(side == 0, core, 1 - core) * (piece * PIECES)
            for p in range(PIECES):
                both = jnp.dot(x, loaded[side * PIECES + p], preferred_element_type=jnp.float32)
                gate, up = both[:, :piece], both[:, piece:]
                value = gate / (1.0 + jnp.exp(-gate)) * up
                hidden[at, pl.ds(pl.multiple_of(start + p * piece, 128), piece)] = value.astype(jnp.bfloat16)
        return carry

    lax.fori_loop(0, blocks // 4, step, 0)


def out_kernel(rows, place, hidden, scale, own, other, *outs):
    core = place[1]
    part = own.shape[1]
    for side, w in ((0, own), (1, other)):
        start = pl.multiple_of(jnp.where(side == 0, core, 1 - core) * part, part)
        for c in range(0, part, 256):
            value = jnp.dot(hidden[...], w[:, c : c + 256], preferred_element_type=jnp.float32)
            value = (value * scale[:, :1]).astype(jnp.bfloat16)
            for q in range(4):
                outs[q][:, pl.ds(pl.multiple_of(start + c, 256), 256)] = value[q * rows : (q + 1) * rows]


def local(tokens, route_ids, route_weights, w_gate, w_up, w_down):
    devices = lax.axis_size("expert")
    experts, depth, width = w_gate.shape
    rows, model = tokens.shape
    line = devices // 4
    me = lax.axis_index("expert")
    core = lax.axis_index("dp") % 2
    place = jnp.stack([me, core]).astype(jnp.int32)
    half, part = width // 2, model // 2
    piece = half // PIECES
    f32, bf16 = jnp.float32, jnp.bfloat16

    share = jnp.sum(
        jnp.where(
            route_ids[:, :, None] == jnp.arange(experts, dtype=jnp.int32)[None, None, :],
            route_weights[:, :, None],
            0.0,
        ),
        axis=1,
    )
    first = share.astype(bf16)
    rest = share - first.astype(f32)
    second = rest.astype(bf16)
    third = (rest - second.astype(f32)).astype(bf16)
    extra = jnp.concatenate([first, second, third], axis=1)
    extra = jnp.pad(extra, ((0, 0), (0, -(3 * experts) % 128)))
    tokens = jnp.concatenate([tokens, extra], axis=1)

    held = [tokens]
    for s in range(1, line):
        held.append(turn(held[-1], 1))
    by_x, by_y, across = [], [], []
    for s in range(line):
        by_x.append(flip(held[s], 1))
        by_y.append(flip(held[s], 2))
        across.append(flip(by_x[s], 2) if s % 2 == 0 else flip(by_y[s], 1))

    wides = []
    for p in range(PIECES):
        at = core * half + p * piece
        wide = jnp.concatenate(
            [lax.dynamic_slice_in_dim(w, at, piece, axis=2) for w in (w_gate, w_up)], axis=2
        )
        wide = after(wide, *by_x[:2], *by_y[:2], held[-1])
        wides.append(spread(wide))
    flat = [w.reshape(devices * depth, 2 * piece) for w in wides]
    flat_other = [swap_cores(w) for w in flat]
    down = lax.dynamic_slice_in_dim(w_down, core * part, part, axis=2)
    down = spread(after(down, wides[-1], *by_x[1:], *by_y[1:], *across[:2])).reshape(width, part)
    down_other = swap_cores(down)

    gathered = [b for s in range(line) for b in (held[s], by_x[s], by_y[s], across[s])]
    total_rows = devices * rows
    any_spec = pl.BlockSpec(memory_space=pl.ANY)
    vmem_spec = pl.BlockSpec(memory_space=pltpu.VMEM)
    smem_spec = pl.BlockSpec(memory_space=pltpu.SMEM)
    hidden, scale = pl.pallas_call(
        functools.partial(hidden_kernel, devices, rows, model, experts),
        out_shape=[
            jax.ShapeDtypeStruct((total_rows, width), bf16),
            jax.ShapeDtypeStruct((total_rows, 128), f32),
        ],
        in_specs=[smem_spec] + [any_spec] * (devices + 2 * PIECES),
        out_specs=[vmem_spec, vmem_spec],
        scratch_shapes=[
            pltpu.VMEM((total_rows, tokens.shape[1]), bf16),
            pltpu.VMEM((2 * PIECES, devices * depth, 2 * piece), bf16),
            pltpu.SemaphoreType.DMA((devices,)),
            pltpu.SemaphoreType.DMA((2 * PIECES,)),
        ],
        compiler_params=pltpu.CompilerParams(vmem_limit_bytes=48 * 1024 * 1024),
        cost_estimate=pl.CostEstimate(
            flops=4 * total_rows * model * width, bytes_accessed=20_000_000, transcendentals=total_rows * width
        ),
        name="hidden",
    )(place, *gathered, *flat, *flat_other)

    group = 4 * rows
    arriving = None
    for s in reversed(range(line)):
        kept, to_x, to_y, over = pl.pallas_call(
            functools.partial(out_kernel, rows),
            out_shape=[jax.ShapeDtypeStruct((rows, model), bf16)] * 4,
            grid=(1,),
            in_specs=[
                smem_spec,
                pl.BlockSpec((group, width), lambda i, s=s: (s, 0)),
                pl.BlockSpec((group, 128), lambda i, s=s: (s, 0)),
                pl.BlockSpec((width, part), lambda i: (0, 0)),
                pl.BlockSpec((width, part), lambda i: (0, 0)),
            ],
            out_specs=[pl.BlockSpec((rows, model), lambda i: (0, 0))] * 4,
            compiler_params=pltpu.CompilerParams(vmem_limit_bytes=32 * 1024 * 1024),
            cost_estimate=pl.CostEstimate(
                flops=2 * group * model * width, bytes_accessed=6_500_000, transcendentals=0
            ),
            name="out",
        )(place, hidden, scale, down, down_other)
        if s % 2 == 0:
            to_x = (to_x.astype(f32) + flip(over, 2).astype(f32)).astype(bf16)
        else:
            to_y = (to_y.astype(f32) + flip(over, 1).astype(f32)).astype(bf16)
        total = kept.astype(f32) + flip(to_x, 1).astype(f32) + flip(to_y, 2).astype(f32)
        if arriving is not None:
            total = total + arriving.astype(f32)
        if s > 0:
            arriving = turn(total.astype(bf16), -1)
    return total.astype(bf16)


def solution(mesh):
    placed = (
        P(("dp", "expert"), None),
        P(("dp", "expert"), None),
        P(("dp", "expert"), None),
        P(None, "expert", None),
        P(None, "expert", None),
        P(None, "expert", None),
    )
    return jax.shard_map(
        local, mesh=mesh, in_specs=placed, out_specs=P(("dp", "expert"), None), check_vma=False
    )
```

```python
import functools

import jax
import jax.numpy as jnp
from jax import lax
from jax.experimental import pallas as pl
from jax.experimental.pallas import tpu as pltpu
from jax.sharding import PartitionSpec as P

def swap_cores(x):
    size = lax.axis_size("dp")
    return lax.ppermute(x, "dp", [(i, i ^ 1) for i in range(size)])


def flip(x, bit):
    size = lax.axis_size("expert")
    return lax.ppermute(x, "expert", [(i, i ^ bit) for i in range(size)])


def turn(x, by):
    size = lax.axis_size("expert")
    return lax.ppermute(x, "expert", [(i, (i + 4 * by) % size) for i in range(size)])


def spread(w):
    return lax.all_to_all(w, "expert", split_axis=0, concat_axis=0, tiled=True)


def after(x, *others):
    return lax.optimization_barrier((x, *others))[0]


def hidden_kernel(blocks, rows, model, experts, place, *refs):
    tokens, weights = refs[:blocks], refs[blocks : blocks + 2]
    hidden, scale, held, loaded, token_sems, weight_sems = refs[blocks + 2 :]
    me, core = place[0], place[1]
    token_copies = [
        pltpu.make_async_copy(tokens[i], held.at[pl.ds(i * rows, rows)], token_sems.at[i]) for i in range(blocks)
    ]
    weight_copies = [pltpu.make_async_copy(weights[i], loaded.at[i], weight_sems.at[i]) for i in range(2)]
    for copy in token_copies[:4]:
        copy.start()
    weight_copies[0].start()
    for copy in token_copies[4:]:
        copy.start()
    weight_copies[1].start()
    group = 4 * rows
    piece = loaded.shape[2] // 2
    columns = held.shape[1] - model
    for side in range(2):
        start = pl.multiple_of(jnp.where(side == 0, core, 1 - core) * piece, 128)
        weight_copies[side].wait()
        for s in range(blocks // 4):
            if side == 0:
                for copy in token_copies[4 * s : 4 * s + 4]:
                    copy.wait()
            for half in range(2):
                at = pl.ds(s * group + half * group // 2, group // 2)
                if side == 0:
                    lane = lax.broadcasted_iota(jnp.int32, (group // 2, columns), 1)
                    wanted = (lane == me) | (lane == me + experts) | (lane == me + 2 * experts)
                    picked = jnp.where(wanted, held[at, model:].astype(jnp.float32), 0.0)
                    scale[at, :] = jnp.broadcast_to(jnp.sum(picked, axis=1, keepdims=True), (group // 2, 128))
                both = jnp.dot(held[at, :model], loaded[side], preferred_element_type=jnp.float32)
                gate, up = both[:, :piece], both[:, piece:]
                value = gate / (1.0 + jnp.exp(-gate)) * up
                hidden[at, pl.ds(start, piece)] = value.astype(jnp.bfloat16)


def out_kernel(rows, place, hidden, scale, own, other, *outs):
    core = place[1]
    part = own.shape[1]
    for side, w in ((0, own), (1, other)):
        start = pl.multiple_of(jnp.where(side == 0, core, 1 - core) * part, part)
        for c in range(0, part, 256):
            value = jnp.dot(hidden[...], w[:, c : c + 256], preferred_element_type=jnp.float32)
            value = (value * scale[:, :1]).astype(jnp.bfloat16)
            for q in range(4):
                outs[q][:, pl.ds(pl.multiple_of(start + c, 256), 256)] = value[q * rows : (q + 1) * rows]


def local(tokens, route_ids, route_weights, w_gate, w_up, w_down):
    devices = lax.axis_size("expert")
    experts, depth, width = w_gate.shape
    rows, model = tokens.shape
    line = devices // 4
    me = lax.axis_index("expert")
    core = lax.axis_index("dp") % 2
    place = jnp.stack([me, core]).astype(jnp.int32)
    half, part = width // 2, model // 2
    f32, bf16 = jnp.float32, jnp.bfloat16

    share = jnp.sum(
        jnp.where(
            route_ids[:, :, None] == jnp.arange(experts, dtype=jnp.int32)[None, None, :],
            route_weights[:, :, None],
            0.0,
        ),
        axis=1,
    )
    first = share.astype(bf16)
    rest = share - first.astype(f32)
    second = rest.astype(bf16)
    third = (rest - second.astype(f32)).astype(bf16)
    extra = jnp.concatenate([first, second, third], axis=1)
    extra = jnp.pad(extra, ((0, 0), (0, -(3 * experts) % 128)))
    tokens = jnp.concatenate([tokens, extra], axis=1)

    held, by_x, by_y, across = [tokens] + [None] * (line - 1), [None] * line, [None] * line, [None] * line

    def near(s):
        by_x[s], by_y[s] = flip(held[s], 1), flip(held[s], 2)

    def far(s):
        across[s] = flip(by_x[s], 2) if s % 2 == 0 else flip(by_y[s], 1)

    def settle(*extra):
        done = lax.optimization_barrier((held, by_x, by_y, across, extra))
        held[:], by_x[:], by_y[:], across[:] = done[:4]
        return done[4]

    at = core * half
    wide = jnp.concatenate([lax.dynamic_slice_in_dim(w, at, half, axis=2) for w in (w_gate, w_up)], axis=2)
    down = lax.dynamic_slice_in_dim(w_down, core * part, part, axis=2)
    for s in range(1, line):
        held[s] = turn(held[s - 1], 1)
        near(s - 1)
        wide, down = settle(wide, down)
    near(line - 1)
    for s in range(line - 1):
        far(s)
    wide = spread(wide)
    wide, down = settle(wide.reshape(devices * depth, width), down)
    down = spread(down)
    far(line - 1)
    wide_other = swap_cores(wide)
    down = down.reshape(width, part)

    any_spec = pl.BlockSpec(memory_space=pl.ANY)
    vmem_spec = pl.BlockSpec(memory_space=pltpu.VMEM)
    smem_spec = pl.BlockSpec(memory_space=pltpu.SMEM)
    group = 4 * rows

    def hidden_of(places):
        gathered = [b for s in places for b in (held[s], by_x[s], by_y[s], across[s])]
        count = len(gathered) * rows
        return pl.pallas_call(
            functools.partial(hidden_kernel, len(gathered), rows, model, experts),
            out_shape=[
                jax.ShapeDtypeStruct((count, width), bf16),
                jax.ShapeDtypeStruct((count, 128), f32),
            ],
            in_specs=[smem_spec] + [any_spec] * (len(gathered) + 2),
            out_specs=[vmem_spec, vmem_spec],
            scratch_shapes=[
                pltpu.VMEM((count, tokens.shape[1]), bf16),
                pltpu.VMEM((2, devices * depth, width), bf16),
                pltpu.SemaphoreType.DMA((len(gathered),)),
                pltpu.SemaphoreType.DMA((2,)),
            ],
            compiler_params=pltpu.CompilerParams(vmem_limit_bytes=48 * 1024 * 1024),
            cost_estimate=pl.CostEstimate(
                flops=4 * count * model * width, bytes_accessed=10_000_000, transcendentals=count * width
            ),
            name="hidden",
        )(place, *gathered, wide, wide_other)

    hidden, scale = {}, {}

    def work(places):
        h, w = hidden_of(places)
        for i, s in enumerate(places):
            hidden[s], scale[s] = (h, i), (w, i)
        return h

    first = work(range(line - 1))
    wide, wide_other = lax.optimization_barrier((wide, wide_other, first))[:2]
    second = work(range(line - 1, line))
    down_other = swap_cores(after(down, second))
    outs = [None] * line
    for s in reversed(range(line)):
        outs[s] = pl.pallas_call(
            functools.partial(out_kernel, rows),
            out_shape=[jax.ShapeDtypeStruct((rows, model), bf16)] * 4,
            grid=(1,),
            in_specs=[
                smem_spec,
                pl.BlockSpec((group, width), lambda i, s=hidden[s][1]: (s, 0)),
                pl.BlockSpec((group, 128), lambda i, s=scale[s][1]: (s, 0)),
                pl.BlockSpec((width, part), lambda i: (0, 0)),
                pl.BlockSpec((width, part), lambda i: (0, 0)),
            ],
            out_specs=[pl.BlockSpec((rows, model), lambda i: (0, 0))] * 4,
            compiler_params=pltpu.CompilerParams(vmem_limit_bytes=32 * 1024 * 1024),
            cost_estimate=pl.CostEstimate(
                flops=2 * group * model * width, bytes_accessed=6_500_000, transcendentals=0
            ),
            name="out",
        )(place, hidden[s][0], scale[s][0], down, down_other)
    def add(*terms):
        return sum(term.astype(f32) for term in terms).astype(bf16)

    beside = [None] * line
    for s in range(1, line, 2):
        beside[s] = turn(outs[s][3], -1)
    total = None
    from_x, from_y = [None] * line, [None] * line
    for s in reversed(range(line)):
        kept, to_x, to_y, over = outs[s]
        if s % 2 == 0 and s + 1 < line:
            over = add(over, beside[s + 1])
        if s % 4 == 0:
            to_x = add(to_x, flip(over, 2))
        elif s % 2 == 0:
            to_y = add(to_y, flip(over, 1))
        from_x[s], from_y[s] = flip(to_x, 1), flip(to_y, 2)
    for s in reversed(range(line)):
        terms = [outs[s][0], from_x[s], from_y[s]]
        total = add(*terms) if s == line - 1 else add(*terms, turn(total, -1))
    return total


def solution(mesh):
    placed = (
        P(("dp", "expert"), None),
        P(("dp", "expert"), None),
        P(("dp", "expert"), None),
        P(None, "expert", None),
        P(None, "expert", None),
        P(None, "expert", None),
    )
    return jax.shard_map(
        local, mesh=mesh, in_specs=placed, out_specs=P(("dp", "expert"), None), check_vma=False
    )
```

```python
import functools

import jax
import jax.numpy as jnp
from jax import lax
from jax.experimental import pallas as pl
from jax.experimental.pallas import tpu as pltpu
from jax.sharding import PartitionSpec as P

def swap_cores(x):
    size = lax.axis_size("dp")
    return lax.ppermute(x, "dp", [(i, i ^ 1) for i in range(size)])


def flip(x, bit):
    size = lax.axis_size("expert")
    return lax.ppermute(x, "expert", [(i, i ^ bit) for i in range(size)])


def turn(x, by):
    size = lax.axis_size("expert")
    return lax.ppermute(x, "expert", [(i, (i + 4 * by) % size) for i in range(size)])


def spread(w):
    return lax.all_to_all(w, "expert", split_axis=0, concat_axis=0, tiled=True)


def after(x, *others):
    return lax.optimization_barrier((x, *others))[0]


def hidden_kernel(blocks, rows, model, experts, place, *refs):
    tokens, weights = refs[:blocks], refs[blocks : blocks + 2]
    hidden, scale, held, loaded, token_sems, weight_sems = refs[blocks + 2 :]
    me, core = place[0], place[1]
    token_copies = [
        pltpu.make_async_copy(tokens[i], held.at[pl.ds(i * rows, rows)], token_sems.at[i]) for i in range(blocks)
    ]
    weight_copies = [pltpu.make_async_copy(weights[i], loaded.at[i], weight_sems.at[i]) for i in range(2)]
    for copy in token_copies[:4]:
        copy.start()
    weight_copies[0].start()
    for copy in token_copies[4:]:
        copy.start()
    weight_copies[1].start()
    group = 4 * rows
    piece = loaded.shape[2] // 2
    columns = held.shape[1] - model
    for side in range(2):
        start = pl.multiple_of(jnp.where(side == 0, core, 1 - core) * piece, 128)
        weight_copies[side].wait()
        for s in range(blocks // 4):
            if side == 0:
                for copy in token_copies[4 * s : 4 * s + 4]:
                    copy.wait()
            for half in range(2):
                at = pl.ds(s * group + half * group // 2, group // 2)
                if side == 0:
                    lane = lax.broadcasted_iota(jnp.int32, (group // 2, columns), 1)
                    wanted = (lane == me) | (lane == me + experts) | (lane == me + 2 * experts)
                    picked = jnp.where(wanted, held[at, model:].astype(jnp.float32), 0.0)
                    scale[at, :] = jnp.broadcast_to(jnp.sum(picked, axis=1, keepdims=True), (group // 2, 128))
                both = jnp.dot(held[at, :model], loaded[side], preferred_element_type=jnp.float32)
                gate, up = both[:, :piece], both[:, piece:]
                value = gate / (1.0 + jnp.exp(-gate)) * up
                hidden[at, pl.ds(start, piece)] = value.astype(jnp.bfloat16)


def out_kernel(rows, place, hidden, scale, own, other, *outs):
    core = place[1]
    part = own.shape[1]
    for side, w in ((0, own), (1, other)):
        start = pl.multiple_of(jnp.where(side == 0, core, 1 - core) * part, part)
        for c in range(0, part, 256):
            value = jnp.dot(hidden[...], w[:, c : c + 256], preferred_element_type=jnp.float32)
            value = (value * scale[:, :1]).astype(jnp.bfloat16)
            for q in range(4):
                outs[q][:, pl.ds(pl.multiple_of(start + c, 256), 256)] = value[q * rows : (q + 1) * rows]


def local(tokens, route_ids, route_weights, w_gate, w_up, w_down):
    devices = lax.axis_size("expert")
    experts, depth, width = w_gate.shape
    rows, model = tokens.shape
    line = devices // 4
    me = lax.axis_index("expert")
    core = lax.axis_index("dp") % 2
    place = jnp.stack([me, core]).astype(jnp.int32)
    half, part = width // 2, model // 2
    f32, bf16 = jnp.float32, jnp.bfloat16

    share = jnp.sum(
        jnp.where(
            route_ids[:, :, None] == jnp.arange(experts, dtype=jnp.int32)[None, None, :],
            route_weights[:, :, None],
            0.0,
        ),
        axis=1,
    )
    first = share.astype(bf16)
    rest = share - first.astype(f32)
    second = rest.astype(bf16)
    third = (rest - second.astype(f32)).astype(bf16)
    extra = jnp.concatenate([first, second, third], axis=1)
    extra = jnp.pad(extra, ((0, 0), (0, -(3 * experts) % 128)))
    tokens = jnp.concatenate([tokens, extra], axis=1)

    held, by_x, by_y, across = [tokens] + [None] * (line - 1), [None] * line, [None] * line, [None] * line

    def near(s):
        by_x[s], by_y[s] = flip(held[s], 1), flip(held[s], 2)

    def far(s):
        across[s] = flip(by_x[s], 2) if s % 2 == 0 else flip(by_y[s], 1)

    def settle(*extra):
        done = lax.optimization_barrier((held, by_x, by_y, across, extra))
        held[:], by_x[:], by_y[:], across[:] = done[:4]
        return done[4]

    at = core * half
    wide = jnp.concatenate([lax.dynamic_slice_in_dim(w, at, half, axis=2) for w in (w_gate, w_up)], axis=2)
    down = lax.dynamic_slice_in_dim(w_down, core * part, part, axis=2)
    for s in range(1, line):
        held[s] = turn(held[s - 1], 1)
        near(s - 1)
        wide, down = settle(wide, down)
    near(line - 1)
    for s in range(line - 1):
        far(s)
    wide = spread(wide)
    wide, down = settle(wide.reshape(devices * depth, width), down)
    down = spread(down)
    far(line - 1)
    wide_other = swap_cores(wide)
    down = down.reshape(width, part)

    any_spec = pl.BlockSpec(memory_space=pl.ANY)
    vmem_spec = pl.BlockSpec(memory_space=pltpu.VMEM)
    smem_spec = pl.BlockSpec(memory_space=pltpu.SMEM)
    group = 4 * rows

    def hidden_of(places):
        gathered = [b for s in places for b in (held[s], by_x[s], by_y[s], across[s])]
        count = len(gathered) * rows
        return pl.pallas_call(
            functools.partial(hidden_kernel, len(gathered), rows, model, experts),
            out_shape=[
                jax.ShapeDtypeStruct((count, width), bf16),
                jax.ShapeDtypeStruct((count, 128), f32),
            ],
            in_specs=[smem_spec] + [any_spec] * (len(gathered) + 2),
            out_specs=[vmem_spec, vmem_spec],
            scratch_shapes=[
                pltpu.VMEM((count, tokens.shape[1]), bf16),
                pltpu.VMEM((2, devices * depth, width), bf16),
                pltpu.SemaphoreType.DMA((len(gathered),)),
                pltpu.SemaphoreType.DMA((2,)),
            ],
            compiler_params=pltpu.CompilerParams(vmem_limit_bytes=48 * 1024 * 1024),
            cost_estimate=pl.CostEstimate(
                flops=4 * count * model * width, bytes_accessed=10_000_000, transcendentals=count * width
            ),
            name="hidden",
        )(place, *gathered, wide, wide_other)

    hidden, scale = {}, {}

    def work(places):
        h, w = hidden_of(places)
        for i, s in enumerate(places):
            hidden[s], scale[s] = (h, i), (w, i)
        return h

    first = work(range(line - 1))
    wide, wide_other = lax.optimization_barrier((wide, wide_other, first))[:2]
    second = work(range(line - 1, line))
    down_other = swap_cores(after(down, second))
    outs = [None] * line
    for s in [*range(line - 1, 0, -2), *range(line - 2, -1, -2)]:
        outs[s] = pl.pallas_call(
            functools.partial(out_kernel, rows),
            out_shape=[jax.ShapeDtypeStruct((rows, model), bf16)] * 4,
            grid=(1,),
            in_specs=[
                smem_spec,
                pl.BlockSpec((group, width), lambda i, s=hidden[s][1]: (s, 0)),
                pl.BlockSpec((group, 128), lambda i, s=scale[s][1]: (s, 0)),
                pl.BlockSpec((width, part), lambda i: (0, 0)),
                pl.BlockSpec((width, part), lambda i: (0, 0)),
            ],
            out_specs=[pl.BlockSpec((rows, model), lambda i: (0, 0))] * 4,
            compiler_params=pltpu.CompilerParams(vmem_limit_bytes=32 * 1024 * 1024),
            cost_estimate=pl.CostEstimate(
                flops=2 * group * model * width, bytes_accessed=6_500_000, transcendentals=0
            ),
            name="out",
        )(place, hidden[s][0], scale[s][0], down, down_other)
    def add(*terms):
        return sum(term.astype(f32) for term in terms).astype(bf16)

    beside, corner = [None] * line, [None] * line
    for s in reversed(range(1, line, 2)):
        beside[s] = turn(outs[s][3], -1)
    from_x, from_y = [None] * line, [None] * line
    for s in reversed(range(0, line, 2)):
        over = add(outs[s][3], beside[s + 1]) if s + 1 < line else outs[s][3]
        corner[s] = flip(over, 2 if s % 4 == 0 else 1)
    early = beside[line - 1]
    for s in reversed(range(line)):
        kept, to_x, to_y, over = outs[s]
        if s % 2 == 1:
            if s < line - 1:
                to_x, to_y = after(to_x, early), to_y
        elif s % 4 == 0:
            to_x, to_y = add(to_x, corner[s]), after(to_y, early)
        else:
            to_x, to_y = after(to_x, early), add(to_y, corner[s])
        from_x[s], from_y[s] = flip(to_x, 1), flip(to_y, 2)
    total = add(outs[line - 1][0], from_x[line - 1], from_y[line - 1])
    for s in reversed(range(line - 1)):
        total = add(outs[s][0], from_x[s], from_y[s], turn(total, -1))
    return total


def solution(mesh):
    placed = (
        P(("dp", "expert"), None),
        P(("dp", "expert"), None),
        P(("dp", "expert"), None),
        P(None, "expert", None),
        P(None, "expert", None),
        P(None, "expert", None),
    )
    return jax.shard_map(
        local, mesh=mesh, in_specs=placed, out_specs=P(("dp", "expert"), None), check_vma=False
    )
```

```python
import functools

import jax
import jax.numpy as jnp
from jax import lax
from jax.experimental import pallas as pl
from jax.experimental.pallas import tpu as pltpu
from jax.sharding import PartitionSpec as P

def swap_cores(x):
    size = lax.axis_size("dp")
    return lax.ppermute(x, "dp", [(i, i ^ 1) for i in range(size)])


def flip(x, bit):
    size = lax.axis_size("expert")
    return lax.ppermute(x, "expert", [(i, i ^ bit) for i in range(size)])


def turn(x, by):
    size = lax.axis_size("expert")
    return lax.ppermute(x, "expert", [(i, (i + 4 * by) % size) for i in range(size)])


def spread(w):
    return lax.all_to_all(w, "expert", split_axis=0, concat_axis=0, tiled=True)


def after(x, *others):
    return lax.optimization_barrier((x, *others))[0]


def hidden_kernel(blocks, rows, model, experts, place, *refs):
    tokens, weights = refs[:blocks], refs[blocks : blocks + 2]
    hidden, scale, held, loaded, token_sems, weight_sems = refs[blocks + 2 :]
    me, core = place[0], place[1]
    token_copies = [
        pltpu.make_async_copy(tokens[i], held.at[pl.ds(i * rows, rows)], token_sems.at[i]) for i in range(blocks)
    ]
    weight_copies = [pltpu.make_async_copy(weights[i], loaded.at[i], weight_sems.at[i]) for i in range(2)]
    for copy in token_copies[:4]:
        copy.start()
    weight_copies[0].start()
    for copy in token_copies[4:]:
        copy.start()
    weight_copies[1].start()
    group = 4 * rows
    piece = loaded.shape[2] // 2
    columns = held.shape[1] - model
    for side in range(2):
        start = pl.multiple_of(jnp.where(side == 0, core, 1 - core) * piece, 128)
        weight_copies[side].wait()
        for s in range(blocks // 4):
            if side == 0:
                for copy in token_copies[4 * s : 4 * s + 4]:
                    copy.wait()
            for half in range(2):
                at = pl.ds(s * group + half * group // 2, group // 2)
                if side == 0:
                    lane = lax.broadcasted_iota(jnp.int32, (group // 2, columns), 1)
                    wanted = (lane == me) | (lane == me + experts) | (lane == me + 2 * experts)
                    picked = jnp.where(wanted, held[at, model:].astype(jnp.float32), 0.0)
                    scale[at, :] = jnp.broadcast_to(jnp.sum(picked, axis=1, keepdims=True), (group // 2, 128))
                both = jnp.dot(held[at, :model], loaded[side], preferred_element_type=jnp.float32)
                gate, up = both[:, :piece], both[:, piece:]
                value = gate / (1.0 + jnp.exp(-gate)) * up
                hidden[at, pl.ds(start, piece)] = value.astype(jnp.bfloat16)


def out_kernel(rows, place, hidden, scale, own, other, *outs):
    core = place[1]
    part = own.shape[1]
    for side, w in ((0, own), (1, other)):
        start = pl.multiple_of(jnp.where(side == 0, core, 1 - core) * part, part)
        for c in range(0, part, 256):
            value = jnp.dot(hidden[...], w[:, c : c + 256], preferred_element_type=jnp.float32)
            value = (value * scale[:, :1]).astype(jnp.bfloat16)
            for q in range(4):
                outs[q][:, pl.ds(pl.multiple_of(start + c, 256), 256)] = value[q * rows : (q + 1) * rows]


def local(tokens, route_ids, route_weights, w_gate, w_up, w_down):
    devices = lax.axis_size("expert")
    experts, depth, width = w_gate.shape
    rows, model = tokens.shape
    line = devices // 4
    me = lax.axis_index("expert")
    core = lax.axis_index("dp") % 2
    place = jnp.stack([me, core]).astype(jnp.int32)
    half, part = width // 2, model // 2
    f32, bf16 = jnp.float32, jnp.bfloat16

    share = jnp.sum(
        jnp.where(
            route_ids[:, :, None] == jnp.arange(experts, dtype=jnp.int32)[None, None, :],
            route_weights[:, :, None],
            0.0,
        ),
        axis=1,
    )
    first = share.astype(bf16)
    rest = share - first.astype(f32)
    second = rest.astype(bf16)
    third = (rest - second.astype(f32)).astype(bf16)
    extra = jnp.concatenate([first, second, third], axis=1)
    extra = jnp.pad(extra, ((0, 0), (0, -(3 * experts) % 128)))
    tokens = jnp.concatenate([tokens, extra], axis=1)

    held, by_x, by_y, across = [tokens] + [None] * (line - 1), [None] * line, [None] * line, [None] * line

    def near(s):
        by_x[s], by_y[s] = flip(held[s], 1), flip(held[s], 2)

    def far(s):
        if s != line - 2:
            across[s] = flip(by_x[s], 2) if s % 2 == 0 else flip(by_y[s], 1)
        else:
            cut = rows // 2
            across[s] = jnp.concatenate([flip(by_x[s][:cut], 2), flip(by_y[s][cut:], 1)], axis=0)

    def settle(*extra):
        done = lax.optimization_barrier((held, by_x, by_y, across, extra))
        held[:], by_x[:], by_y[:], across[:] = done[:4]
        return done[4]

    at = core * half
    wide = jnp.concatenate([lax.dynamic_slice_in_dim(w, at, half, axis=2) for w in (w_gate, w_up)], axis=2)
    down = lax.dynamic_slice_in_dim(w_down, core * part, part, axis=2)
    for s in range(1, line):
        held[s] = turn(held[s - 1], 1)
        near(s - 1)
        wide, down = settle(wide, down)
    near(line - 1)
    for s in range(line - 1):
        far(s)
    wide = spread(wide)
    wide, down = settle(wide.reshape(devices * depth, width), down)
    down = spread(down)
    far(line - 1)
    wide_other = swap_cores(wide)
    down = down.reshape(width, part)

    any_spec = pl.BlockSpec(memory_space=pl.ANY)
    vmem_spec = pl.BlockSpec(memory_space=pltpu.VMEM)
    smem_spec = pl.BlockSpec(memory_space=pltpu.SMEM)
    group = 4 * rows

    def hidden_of(places):
        gathered = [b for s in places for b in (held[s], by_x[s], by_y[s], across[s])]
        count = len(gathered) * rows
        return pl.pallas_call(
            functools.partial(hidden_kernel, len(gathered), rows, model, experts),
            out_shape=[
                jax.ShapeDtypeStruct((count, width), bf16),
                jax.ShapeDtypeStruct((count, 128), f32),
            ],
            in_specs=[smem_spec] + [any_spec] * (len(gathered) + 2),
            out_specs=[vmem_spec, vmem_spec],
            scratch_shapes=[
                pltpu.VMEM((count, tokens.shape[1]), bf16),
                pltpu.VMEM((2, devices * depth, width), bf16),
                pltpu.SemaphoreType.DMA((len(gathered),)),
                pltpu.SemaphoreType.DMA((2,)),
            ],
            compiler_params=pltpu.CompilerParams(vmem_limit_bytes=48 * 1024 * 1024),
            cost_estimate=pl.CostEstimate(
                flops=4 * count * model * width, bytes_accessed=10_000_000, transcendentals=count * width
            ),
            name="hidden",
        )(place, *gathered, wide, wide_other)

    hidden, scale = {}, {}

    def work(places):
        h, w = hidden_of(places)
        for i, s in enumerate(places):
            hidden[s], scale[s] = (h, i), (w, i)
        return h

    first = work(range(line - 1))
    wide, wide_other = lax.optimization_barrier((wide, wide_other, first))[:2]
    second = work(range(line - 1, line))
    down_other = swap_cores(after(down, second))
    outs = [None] * line
    for s in [*range(line - 1, 0, -2), *range(line - 2, -1, -2)]:
        outs[s] = pl.pallas_call(
            functools.partial(out_kernel, rows),
            out_shape=[jax.ShapeDtypeStruct((rows, model), bf16)] * 4,
            grid=(1,),
            in_specs=[
                smem_spec,
                pl.BlockSpec((group, width), lambda i, s=hidden[s][1]: (s, 0)),
                pl.BlockSpec((group, 128), lambda i, s=scale[s][1]: (s, 0)),
                pl.BlockSpec((width, part), lambda i: (0, 0)),
                pl.BlockSpec((width, part), lambda i: (0, 0)),
            ],
            out_specs=[pl.BlockSpec((rows, model), lambda i: (0, 0))] * 4,
            compiler_params=pltpu.CompilerParams(vmem_limit_bytes=32 * 1024 * 1024),
            cost_estimate=pl.CostEstimate(
                flops=2 * group * model * width, bytes_accessed=6_500_000, transcendentals=0
            ),
            name="out",
        )(place, hidden[s][0], scale[s][0], down, down_other)
    def add(*terms):
        return sum(term.astype(f32) for term in terms).astype(bf16)

    beside, corner = [None] * line, [None] * line
    for s in reversed(range(1, line, 2)):
        beside[s] = turn(outs[s][3], -1)
    from_x, from_y = [None] * line, [None] * line
    for s in reversed(range(0, line, 2)):
        over = add(outs[s][3], beside[s + 1]) if s + 1 < line else outs[s][3]
        corner[s] = flip(over, 2 if s % 4 == 0 else 1)
    early = beside[line - 1]
    for s in reversed(range(line)):
        kept, to_x, to_y, over = outs[s]
        if s % 2 == 1:
            if s < line - 1:
                to_x, to_y = after(to_x, early), to_y
        elif s % 4 == 0:
            to_x, to_y = add(to_x, corner[s]), after(to_y, early)
        else:
            to_x, to_y = after(to_x, early), add(to_y, corner[s])
        from_x[s], from_y[s] = flip(to_x, 1), flip(to_y, 2)
    total = add(outs[line - 1][0], from_x[line - 1], from_y[line - 1])
    for s in reversed(range(line - 1)):
        total = add(outs[s][0], from_x[s], from_y[s], turn(total, -1))
    return total


def solution(mesh):
    placed = (
        P(("dp", "expert"), None),
        P(("dp", "expert"), None),
        P(("dp", "expert"), None),
        P(None, "expert", None),
        P(None, "expert", None),
        P(None, "expert", None),
    )
    return jax.shard_map(
        local, mesh=mesh, in_specs=placed, out_specs=P(("dp", "expert"), None), check_vma=False
    )
```

```python
import functools

import jax
import jax.numpy as jnp
from jax import lax
from jax.experimental import pallas as pl
from jax.experimental.pallas import tpu as pltpu
from jax.sharding import PartitionSpec as P

def swap_cores(x):
    size = lax.axis_size("dp")
    return lax.ppermute(x, "dp", [(i, i ^ 1) for i in range(size)])


def flip(x, bit):
    size = lax.axis_size("expert")
    return lax.ppermute(x, "expert", [(i, i ^ bit) for i in range(size)])


def turn(x, by):
    size = lax.axis_size("expert")
    return lax.ppermute(x, "expert", [(i, (i + 4 * by) % size) for i in range(size)])


def spread(w):
    return lax.all_to_all(w, "expert", split_axis=0, concat_axis=0, tiled=True)


def after(x, *others):
    return lax.optimization_barrier((x, *others))[0]


def hidden_kernel(blocks, rows, model, experts, place, *refs):
    tokens, weights = refs[:blocks], refs[blocks : blocks + 2]
    hidden, scale, held, loaded, token_sems, weight_sems = refs[blocks + 2 :]
    me, core = place[0], place[1]
    token_copies = [
        pltpu.make_async_copy(tokens[i], held.at[pl.ds(i * rows, rows)], token_sems.at[i]) for i in range(blocks)
    ]
    weight_copies = [pltpu.make_async_copy(weights[i], loaded.at[i], weight_sems.at[i]) for i in range(2)]
    for copy in token_copies[:4]:
        copy.start()
    weight_copies[0].start()
    for copy in token_copies[4:]:
        copy.start()
    weight_copies[1].start()
    group = 4 * rows
    piece = loaded.shape[2] // 2
    columns = held.shape[1] - model
    for side in range(2):
        start = pl.multiple_of(jnp.where(side == 0, core, 1 - core) * piece, 128)
        weight_copies[side].wait()
        for s in range(blocks // 4):
            if side == 0:
                for copy in token_copies[4 * s : 4 * s + 4]:
                    copy.wait()
            for half in range(2):
                at = pl.ds(s * group + half * group // 2, group // 2)
                if side == 0:
                    lane = lax.broadcasted_iota(jnp.int32, (group // 2, columns), 1)
                    wanted = (lane == me) | (lane == me + experts) | (lane == me + 2 * experts)
                    picked = jnp.where(wanted, held[at, model:].astype(jnp.float32), 0.0)
                    scale[at, :] = jnp.broadcast_to(jnp.sum(picked, axis=1, keepdims=True), (group // 2, 128))
                both = jnp.dot(held[at, :model], loaded[side], preferred_element_type=jnp.float32)
                gate, up = both[:, :piece], both[:, piece:]
                value = gate / (1.0 + jnp.exp(-gate)) * up
                hidden[at, pl.ds(start, piece)] = value.astype(jnp.bfloat16)


def out_kernel(rows, place, hidden, scale, own, other, *outs):
    core = place[1]
    part = own.shape[1]
    for side, w in ((0, own), (1, other)):
        start = pl.multiple_of(jnp.where(side == 0, core, 1 - core) * part, part)
        for c in range(0, part, 256):
            value = jnp.dot(hidden[...], w[:, c : c + 256], preferred_element_type=jnp.float32)
            value = (value * scale[:, :1]).astype(jnp.bfloat16)
            for q in range(4):
                outs[q][:, pl.ds(pl.multiple_of(start + c, 256), 256)] = value[q * rows : (q + 1) * rows]


def local(tokens, route_ids, route_weights, w_gate, w_up, w_down):
    devices = lax.axis_size("expert")
    experts, depth, width = w_gate.shape
    rows, model = tokens.shape
    line = devices // 4
    me = lax.axis_index("expert")
    core = lax.axis_index("dp") % 2
    place = jnp.stack([me, core]).astype(jnp.int32)
    half, part = width // 2, model // 2
    f32, bf16 = jnp.float32, jnp.bfloat16

    share = jnp.sum(
        jnp.where(
            route_ids[:, :, None] == jnp.arange(experts, dtype=jnp.int32)[None, None, :],
            route_weights[:, :, None],
            0.0,
        ),
        axis=1,
    )
    first = share.astype(bf16)
    rest = share - first.astype(f32)
    second = rest.astype(bf16)
    third = (rest - second.astype(f32)).astype(bf16)
    extra = jnp.concatenate([first, second, third], axis=1)
    extra = jnp.pad(extra, ((0, 0), (0, -(3 * experts) % 128)))
    tokens = jnp.concatenate([tokens, extra], axis=1)

    held, by_x, by_y, across = [tokens] + [None] * (line - 1), [None] * line, [None] * line, [None] * line

    def near(s):
        by_x[s], by_y[s] = flip(held[s], 1), flip(held[s], 2)

    def far(s):
        if s != line - 2:
            across[s] = flip(by_x[s], 2) if s % 2 == 0 else flip(by_y[s], 1)
        else:
            cut = rows // 2
            across[s] = jnp.concatenate([flip(by_x[s][:cut], 2), flip(by_y[s][cut:], 1)], axis=0)

    def settle(*extra):
        done = lax.optimization_barrier((held, by_x, by_y, across, extra))
        held[:], by_x[:], by_y[:], across[:] = done[:4]
        return done[4]

    at = core * half
    wide = jnp.concatenate([lax.dynamic_slice_in_dim(w, at, half, axis=2) for w in (w_gate, w_up)], axis=2)
    down = lax.dynamic_slice_in_dim(w_down, core * part, part, axis=2)
    for s in range(1, line):
        held[s] = turn(held[s - 1], 1)
        near(s - 1)
        wide, down = settle(wide, down)
    near(line - 1)
    for s in range(line - 1):
        far(s)
    wide = spread(wide)
    wide, down = settle(wide.reshape(devices * depth, width), down)
    down = spread(down)
    far(line - 1)
    wide_other = swap_cores(wide)
    down = down.reshape(width, part)

    any_spec = pl.BlockSpec(memory_space=pl.ANY)
    vmem_spec = pl.BlockSpec(memory_space=pltpu.VMEM)
    smem_spec = pl.BlockSpec(memory_space=pltpu.SMEM)
    group = 4 * rows

    def hidden_of(places):
        gathered = [b for s in places for b in (held[s], by_x[s], by_y[s], across[s])]
        count = len(gathered) * rows
        return pl.pallas_call(
            functools.partial(hidden_kernel, len(gathered), rows, model, experts),
            out_shape=[
                jax.ShapeDtypeStruct((count, width), bf16),
                jax.ShapeDtypeStruct((count, 128), f32),
            ],
            in_specs=[smem_spec] + [any_spec] * (len(gathered) + 2),
            out_specs=[vmem_spec, vmem_spec],
            scratch_shapes=[
                pltpu.VMEM((count, tokens.shape[1]), bf16),
                pltpu.VMEM((2, devices * depth, width), bf16),
                pltpu.SemaphoreType.DMA((len(gathered),)),
                pltpu.SemaphoreType.DMA((2,)),
            ],
            compiler_params=pltpu.CompilerParams(vmem_limit_bytes=48 * 1024 * 1024),
            cost_estimate=pl.CostEstimate(
                flops=4 * count * model * width, bytes_accessed=10_000_000, transcendentals=count * width
            ),
            name="hidden",
        )(place, *gathered, wide, wide_other)

    hidden, scale = {}, {}

    def work(places):
        h, w = hidden_of(places)
        for i, s in enumerate(places):
            hidden[s], scale[s] = (h, i), (w, i)
        return h

    first = work(range(line - 1))
    wide, wide_other = lax.optimization_barrier((wide, wide_other, first))[:2]
    second = work(range(line - 1, line))
    down_other = swap_cores(after(down, second))
    outs = [None] * line
    for s in [*range(line - 1, 0, -2), *range(line - 2, -1, -2)]:
        outs[s] = pl.pallas_call(
            functools.partial(out_kernel, rows),
            out_shape=[jax.ShapeDtypeStruct((rows, model), bf16)] * 4,
            grid=(1,),
            in_specs=[
                smem_spec,
                pl.BlockSpec((group, width), lambda i, s=hidden[s][1]: (s, 0)),
                pl.BlockSpec((group, 128), lambda i, s=scale[s][1]: (s, 0)),
                pl.BlockSpec((width, part), lambda i: (0, 0)),
                pl.BlockSpec((width, part), lambda i: (0, 0)),
            ],
            out_specs=[pl.BlockSpec((rows, model), lambda i: (0, 0))] * 4,
            compiler_params=pltpu.CompilerParams(vmem_limit_bytes=32 * 1024 * 1024),
            cost_estimate=pl.CostEstimate(
                flops=2 * group * model * width, bytes_accessed=6_500_000, transcendentals=0
            ),
            name="out",
        )(place, hidden[s][0], scale[s][0], down, down_other)
    def add(*terms):
        return sum(term.astype(f32) for term in terms).astype(bf16)

    beside, corner = [None] * line, [None] * line
    for s in reversed(range(1, line, 2)):
        beside[s] = turn(outs[s][3], -1)
    beside[-1] = after(beside[-1], *(outs[s][0] for s in range(1, line, 2)))
    from_x, from_y = [None] * line, [None] * line
    for s in reversed(range(0, line, 2)):
        over = add(outs[s][3], beside[s + 1]) if s + 1 < line else outs[s][3]
        corner[s] = flip(over, 2 if s % 4 == 0 else 1)
    early = beside[line - 1]
    for s in reversed(range(line)):
        kept, to_x, to_y, over = outs[s]
        if s % 2 == 1:
            if s < line - 1:
                to_x, to_y = after(to_x, early), to_y
        elif s % 4 == 0:
            to_x, to_y = add(to_x, corner[s]), after(to_y, early)
        else:
            to_x, to_y = after(to_x, early), add(to_y, corner[s])
        from_x[s], from_y[s] = flip(to_x, 1), flip(to_y, 2)
    total = add(outs[line - 1][0], from_x[line - 1], from_y[line - 1])
    for s in reversed(range(line - 1)):
        total = add(outs[s][0], from_x[s], from_y[s], turn(total, -1))
    return total


def solution(mesh):
    placed = (
        P(("dp", "expert"), None),
        P(("dp", "expert"), None),
        P(("dp", "expert"), None),
        P(None, "expert", None),
        P(None, "expert", None),
        P(None, "expert", None),
    )
    return jax.shard_map(
        local, mesh=mesh, in_specs=placed, out_specs=P(("dp", "expert"), None), check_vma=False
    )
```

```python
import functools

import jax
import jax.numpy as jnp
from jax import lax
from jax.experimental import pallas as pl
from jax.experimental.pallas import tpu as pltpu
from jax.sharding import PartitionSpec as P

def swap_cores(x):
    size = lax.axis_size("dp")
    return lax.ppermute(x, "dp", [(i, i ^ 1) for i in range(size)])


def flip(x, bit):
    size = lax.axis_size("expert")
    return lax.ppermute(x, "expert", [(i, i ^ bit) for i in range(size)])


def turn(x, by):
    size = lax.axis_size("expert")
    return lax.ppermute(x, "expert", [(i, (i + 4 * by) % size) for i in range(size)])


def spread(w):
    return lax.all_to_all(w, "expert", split_axis=0, concat_axis=0, tiled=True)


def after(x, *others):
    return lax.optimization_barrier((x, *others))[0]


def hidden_kernel(blocks, rows, model, experts, place, *refs):
    tokens, weights = refs[:blocks], refs[blocks : blocks + 2]
    hidden, scale, held, loaded, token_sems, weight_sems = refs[blocks + 2 :]
    me, core = place[0], place[1]
    token_copies = [
        pltpu.make_async_copy(tokens[i], held.at[pl.ds(i * rows, rows)], token_sems.at[i]) for i in range(blocks)
    ]
    weight_copies = [pltpu.make_async_copy(weights[i], loaded.at[i], weight_sems.at[i]) for i in range(2)]
    for copy in token_copies[:4]:
        copy.start()
    weight_copies[0].start()
    for copy in token_copies[4:]:
        copy.start()
    weight_copies[1].start()
    group = 4 * rows
    piece = loaded.shape[2] // 2
    columns = held.shape[1] - model
    for side in range(2):
        start = pl.multiple_of(jnp.where(side == 0, core, 1 - core) * piece, 128)
        weight_copies[side].wait()
        for s in range(blocks // 4):
            if side == 0:
                for copy in token_copies[4 * s : 4 * s + 4]:
                    copy.wait()
            for half in range(2):
                at = pl.ds(s * group + half * group // 2, group // 2)
                if side == 0:
                    lane = lax.broadcasted_iota(jnp.int32, (group // 2, columns), 1)
                    wanted = (lane == me) | (lane == me + experts) | (lane == me + 2 * experts)
                    picked = jnp.where(wanted, held[at, model:].astype(jnp.float32), 0.0)
                    scale[at, :] = jnp.broadcast_to(jnp.sum(picked, axis=1, keepdims=True), (group // 2, 128))
                both = jnp.dot(held[at, :model], loaded[side], preferred_element_type=jnp.float32)
                gate, up = both[:, :piece], both[:, piece:]
                value = gate / (1.0 + jnp.exp(-gate)) * up
                hidden[at, pl.ds(start, piece)] = value.astype(jnp.bfloat16)


def out_kernel(rows, count, place, *refs):
    hidden, scale = refs[:count], refs[count : 2 * count]
    own, other = refs[2 * count : 2 * count + 2]
    outs = refs[2 * count + 2 :]
    core = place[1]
    part = own.shape[1]
    for g in range(count):
        for side, w in ((0, own), (1, other)):
            start = pl.multiple_of(jnp.where(side == 0, core, 1 - core) * part, part)
            for c in range(0, part, 256):
                value = jnp.dot(hidden[g][...], w[:, c : c + 256], preferred_element_type=jnp.float32)
                value = (value * scale[g][:, :1]).astype(jnp.bfloat16)
                for q in range(4):
                    out = outs[4 * g + q]
                    out[:, pl.ds(pl.multiple_of(start + c, 256), 256)] = value[q * rows : (q + 1) * rows]


def local(tokens, route_ids, route_weights, w_gate, w_up, w_down):
    devices = lax.axis_size("expert")
    experts, depth, width = w_gate.shape
    rows, model = tokens.shape
    line = devices // 4
    me = lax.axis_index("expert")
    core = lax.axis_index("dp") % 2
    place = jnp.stack([me, core]).astype(jnp.int32)
    half, part = width // 2, model // 2
    f32, bf16 = jnp.float32, jnp.bfloat16

    share = jnp.sum(
        jnp.where(
            route_ids[:, :, None] == jnp.arange(experts, dtype=jnp.int32)[None, None, :],
            route_weights[:, :, None],
            0.0,
        ),
        axis=1,
    )
    first = share.astype(bf16)
    rest = share - first.astype(f32)
    second = rest.astype(bf16)
    third = (rest - second.astype(f32)).astype(bf16)
    extra = jnp.concatenate([first, second, third], axis=1)
    extra = jnp.pad(extra, ((0, 0), (0, -(3 * experts) % 128)))
    tokens = jnp.concatenate([tokens, extra], axis=1)

    held, by_x, by_y, across = [tokens] + [None] * (line - 1), [None] * line, [None] * line, [None] * line

    def near(s):
        by_x[s], by_y[s] = flip(held[s], 1), flip(held[s], 2)

    def far(s):
        if s != line - 2:
            across[s] = flip(by_x[s], 2) if s % 2 == 0 else flip(by_y[s], 1)
        else:
            cut = rows // 2
            across[s] = jnp.concatenate([flip(by_x[s][:cut], 2), flip(by_y[s][cut:], 1)], axis=0)

    def settle(*extra):
        done = lax.optimization_barrier((held, by_x, by_y, across, extra))
        held[:], by_x[:], by_y[:], across[:] = done[:4]
        return done[4]

    at = core * half
    wide = jnp.concatenate([lax.dynamic_slice_in_dim(w, at, half, axis=2) for w in (w_gate, w_up)], axis=2)
    down = lax.dynamic_slice_in_dim(w_down, core * part, part, axis=2)
    for s in range(1, line):
        held[s] = turn(held[s - 1], 1)
        near(s - 1)
        wide, down = settle(wide, down)
    near(line - 1)
    for s in range(line - 1):
        far(s)
    wide = spread(wide)
    wide, down = settle(wide.reshape(devices * depth, width), down)
    down = spread(down)
    far(line - 1)
    wide_other = swap_cores(wide)
    down = down.reshape(width, part)

    any_spec = pl.BlockSpec(memory_space=pl.ANY)
    vmem_spec = pl.BlockSpec(memory_space=pltpu.VMEM)
    smem_spec = pl.BlockSpec(memory_space=pltpu.SMEM)
    group = 4 * rows

    def hidden_of(places):
        gathered = [b for s in places for b in (held[s], by_x[s], by_y[s], across[s])]
        count = len(gathered) * rows
        return pl.pallas_call(
            functools.partial(hidden_kernel, len(gathered), rows, model, experts),
            out_shape=[
                jax.ShapeDtypeStruct((count, width), bf16),
                jax.ShapeDtypeStruct((count, 128), f32),
            ],
            in_specs=[smem_spec] + [any_spec] * (len(gathered) + 2),
            out_specs=[vmem_spec, vmem_spec],
            scratch_shapes=[
                pltpu.VMEM((count, tokens.shape[1]), bf16),
                pltpu.VMEM((2, devices * depth, width), bf16),
                pltpu.SemaphoreType.DMA((len(gathered),)),
                pltpu.SemaphoreType.DMA((2,)),
            ],
            compiler_params=pltpu.CompilerParams(vmem_limit_bytes=48 * 1024 * 1024),
            cost_estimate=pl.CostEstimate(
                flops=4 * count * model * width, bytes_accessed=10_000_000, transcendentals=count * width
            ),
            name="hidden",
        )(place, *gathered, wide, wide_other)

    hidden, scale = {}, {}

    def work(places):
        h, w = hidden_of(places)
        for i, s in enumerate(places):
            hidden[s], scale[s] = (h, i), (w, i)
        return h

    first = work(range(line - 1))
    wide, wide_other = lax.optimization_barrier((wide, wide_other, first))[:2]
    second = work(range(line - 1, line))
    down_other = swap_cores(after(down, second))
    outs = [None] * line
    for places in [[line - 1], *[[s, s - 1] for s in range(line - 2, 0, -2)], [0]]:
        count = len(places)
        made = pl.pallas_call(
            functools.partial(out_kernel, rows, count),
            out_shape=[jax.ShapeDtypeStruct((rows, model), bf16)] * (4 * count),
            grid=(1,),
            in_specs=[smem_spec]
            + [pl.BlockSpec((group, width), lambda i, s=hidden[s][1]: (s, 0)) for s in places]
            + [pl.BlockSpec((group, 128), lambda i, s=scale[s][1]: (s, 0)) for s in places]
            + [pl.BlockSpec((width, part), lambda i: (0, 0))] * 2,
            out_specs=[pl.BlockSpec((rows, model), lambda i: (0, 0))] * (4 * count),
            compiler_params=pltpu.CompilerParams(vmem_limit_bytes=32 * 1024 * 1024),
            cost_estimate=pl.CostEstimate(
                flops=2 * count * group * model * width,
                bytes_accessed=3_200_000 + 3_200_000 * count,
                transcendentals=0,
            ),
            name="out",
        )(place, *[hidden[s][0] for s in places], *[scale[s][0] for s in places], down, down_other)
        for i, s in enumerate(places):
            outs[s] = made[4 * i : 4 * i + 4]

    def add(*terms):
        return sum(term.astype(f32) for term in terms).astype(bf16)

    beside, corner = [None] * line, [None] * line
    for s in reversed(range(1, line, 2)):
        beside[s] = turn(outs[s][3], -1)
    beside[-1] = after(beside[-1], *(outs[s][0] for s in range(1, line, 2)))
    from_x, from_y = [None] * line, [None] * line
    for s in reversed(range(0, line, 2)):
        over = add(outs[s][3], beside[s + 1]) if s + 1 < line else outs[s][3]
        corner[s] = flip(over, 2 if s % 4 == 0 else 1)
    early = beside[line - 1]
    for s in reversed(range(line)):
        kept, to_x, to_y, over = outs[s]
        if s % 2 == 1:
            if s < line - 1:
                to_x, to_y = after(to_x, early), to_y
        elif s % 4 == 0:
            to_x, to_y = add(to_x, corner[s]), after(to_y, early)
        else:
            to_x, to_y = after(to_x, early), add(to_y, corner[s])
        from_x[s], from_y[s] = flip(to_x, 1), flip(to_y, 2)
    total = add(outs[line - 1][0], from_x[line - 1], from_y[line - 1])
    for s in reversed(range(line - 1)):
        total = add(outs[s][0], from_x[s], from_y[s], turn(total, -1))
    return total


def solution(mesh):
    placed = (
        P(("dp", "expert"), None),
        P(("dp", "expert"), None),
        P(("dp", "expert"), None),
        P(None, "expert", None),
        P(None, "expert", None),
        P(None, "expert", None),
    )
    return jax.shard_map(
        local, mesh=mesh, in_specs=placed, out_specs=P(("dp", "expert"), None), check_vma=False
    )
```
